512 devices in a mesh: ctx: 128 (over z, y, core), head: 4 (over x).
Axes of the slice: x: 4, y: 8, z: 8, core: 2. Of those that a mesh axis runs over, the one named last changes fastest.
Arguments:
- queries: bfloat16 [32768, 2048], P('ctx', 'head'), may hold values from -0.4375 to 0.4375
- keys: bfloat16 [32768, 2048], P('ctx', 'head'), may hold values from -0.4375 to 0.4375
- values: bfloat16 [32768, 2048], P('ctx', 'head'), may hold values from -0.4375 to 0.4375
- out_grad: bfloat16 [32768, 2048], P('ctx', 'head'), may hold values from -0.4375 to 0.4375
Outputs:
- query_grad: bfloat16 [32768, 2048], P('ctx', 'head')
- key_grad: bfloat16 [32768, 2048], P('ctx', 'head')
- value_grad: bfloat16 [32768, 2048], P('ctx', 'head')
The draws below stay inside these ranges and needn't reach their ends.
All inputs are finite; a program needn't handle non-finite values.
Results may differ from the reference program's by a relative error of at most 0.0049.
Values sent between devices are 32-bit elements; how exact they have to be, the bound alone decides.
No kernel may reach another device: no remote copies, remote signals or barrier semaphores. Data moves between devices by JAX's collectives and lax.ppermute only.
A program may use at most 128 MiB of HBM per device.

```python
import jax
import jax.numpy as jnp
from jax import lax

HEADS = 32
DH = 64
TOK_DEV = 256
TOKENS = 32768
FEATS = 2048


def levels(stream_key, extent, split, least, top_value):
    factor_of, own = 1.0, jax.random.fold_in(stream_key, 6)
    for position, parts in split:
        steps = jnp.exp(jax.random.uniform(jax.random.fold_in(own, position), (parts,), jnp.float32, least / len(split), top_value / len(split)))
        factor_of = factor_of * jnp.repeat(steps, extent[position] // parts).reshape([-1 if axis == position else 1 for axis in range(len(extent))])
    return factor_of


def gaussian(rng, extent, width, most, split=(), held_as=jnp.bfloat16):
    array = width * jax.random.normal(rng, extent, jnp.float32)
    if split:
        array = array * levels(rng, extent, split, -0.22, 0.18)
    return jnp.clip(array, -most, most).astype(held_as)


def setup_inputs(seed: int = 0) -> dict:
    seeds = jax.random.split(jax.random.key(seed), 5)
    return {
        "queries": gaussian(seeds[0], (TOKENS, FEATS), 0.075, 0.4375, ((0, 128), (1, 4))),
        "keys": gaussian(seeds[1], (TOKENS, FEATS), 0.075, 0.4375, ((0, 128), (1, 4))),
        "values": gaussian(seeds[2], (TOKENS, FEATS), 0.075, 0.4375, ((0, 128), (1, 4))),
        "out_grad": gaussian(seeds[3], (TOKENS, FEATS), 0.075, 0.4375, ((0, 128), (1, 4))),
    }


def block_states(items):
    q, k, v, d = items
    kv = jnp.einsum('thd,the->hde', k, v, precision=lax.Precision.HIGHEST)
    g = jnp.einsum('thd,the->hde', q, d, precision=lax.Precision.HIGHEST)
    return kv, g


def block_grads(items):
    q, k, v, d, prefix, suffix = items
    length = q.shape[0]
    rows = lax.broadcasted_iota(jnp.int32, (length, length), 0)
    cols = lax.broadcasted_iota(jnp.int32, (length, length), 1)
    keep = (rows >= cols).astype(jnp.float32)
    hp = lax.Precision.HIGHEST
    a_score = jnp.einsum('thd,shd->hts', q, k, precision=hp) * keep
    b_score = jnp.einsum('the,she->hts', d, v, precision=hp) * keep
    a_score = a_score.astype(jnp.bfloat16).astype(jnp.float32)
    b_score = b_score.astype(jnp.bfloat16).astype(jnp.float32)
    prefix_r = lax.optimization_barrier(prefix.astype(jnp.bfloat16)).astype(jnp.float32)
    suffix_r = lax.optimization_barrier(suffix.astype(jnp.bfloat16)).astype(jnp.float32)
    dq = jnp.einsum('hts,shd->thd', b_score, k, precision=hp) + jnp.einsum('the,hde->thd', d, prefix_r, precision=hp)
    dk = jnp.einsum('hts,thd->shd', b_score, q, precision=hp) + jnp.einsum('she,hde->shd', v, suffix_r, precision=hp)
    dv = jnp.einsum('hts,the->she', a_score, d, precision=hp) + jnp.einsum('shd,hde->she', k, suffix_r, precision=hp)
    return dq.astype(jnp.bfloat16), dk.astype(jnp.bfloat16), dv.astype(jnp.bfloat16)


def reference(queries, keys, values, out_grad):
    blocks = TOKENS // TOK_DEV

    def view(x):
        return x.astype(jnp.float32).reshape(blocks, TOK_DEV, HEADS, DH)

    q, k, v, d = view(queries), view(keys), view(values), view(out_grad)
    kv, g = lax.map(block_states, (q, k, v, d))
    zeros = jnp.zeros((1, HEADS, DH, DH), jnp.float32)
    prefix = jnp.concatenate([zeros, jnp.cumsum(kv, axis=0)[:-1]], axis=0)
    later = jnp.cumsum(g[::-1], axis=0)[::-1]
    suffix = jnp.concatenate([later[1:], zeros], axis=0)
    dq, dk, dv = lax.map(block_grads, (q, k, v, d, prefix, suffix))
    return (dq.reshape(TOKENS, FEATS), dk.reshape(TOKENS, FEATS), dv.reshape(TOKENS, FEATS))
```

```python
import functools

import jax
import jax.numpy as jnp
from jax import lax
from jax.experimental import pallas as pl
from jax.experimental.pallas import tpu as pltpu
from jax.sharding import PartitionSpec as P

DH = 64
PAIR = 2 * DH
QUAD = 4 * DH
VMEM = pltpu.VMEM
F32 = jnp.float32
BF16 = jnp.bfloat16
NT = (((1,), (1,)), ((), ()))
NN = (((1,), (0,)), ((), ()))
TN = (((0,), (0,)), ((), ()))


def dot(a, b, dims):
    return lax.dot_general(a, b, dims, preferred_element_type=F32)


def low_lanes(shape):
    return (lax.broadcasted_iota(jnp.int32, shape, 1) & DH) == 0


def in_block(q_ref, k_ref, v_ref, d_ref, dq_ref, dk_ref, dv_ref):
    length, width = q_ref.shape
    rows = lax.broadcasted_iota(jnp.int32, (length, length), 0)
    cols = lax.broadcasted_iota(jnp.int32, (length, length), 1)
    keep = rows >= cols
    keep_t = cols >= rows
    low = low_lanes((length, PAIR))
    for p in range(width // PAIR):
        at = pl.ds(p * PAIR, PAIR)
        q, k, v, d = q_ref[:, at], k_ref[:, at], v_ref[:, at], d_ref[:, at]
        dq = dk = dv = 0.0
        for mine in (low, ~low):
            kh = jnp.where(mine, k, 0)
            vh = jnp.where(mine, v, 0)
            qh = jnp.where(mine, q, 0)
            dh = jnp.where(mine, d, 0)
            b = jnp.where(keep, dot(d, vh, NT), 0.0).astype(BF16)
            bt = jnp.where(keep_t, dot(v, dh, NT), 0.0).astype(BF16)
            at_ = jnp.where(keep_t, dot(k, qh, NT), 0.0).astype(BF16)
            dq += dot(b, kh, NN)
            dk += dot(bt, qh, NN)
            dv += dot(at_, dh, NN)
        dq_ref[:, at] = dq
        dk_ref[:, at] = dk
        dv_ref[:, at] = dv


def packed_state(a_ref, b_ref, out_ref, base):
    width = a_ref.shape[1]
    low = low_lanes((DH, PAIR))
    for g in range(width // QUAD):
        at = pl.ds(g * QUAD, QUAD)
        full = dot(a_ref[:, at], b_ref[:, at], TN)
        for j in range(2):
            lanes = slice(j * PAIR, (j + 1) * PAIR)
            top = full[j * PAIR : j * PAIR + DH, lanes]
            bottom = full[j * PAIR + DH : (j + 1) * PAIR, lanes]
            out_ref[pl.ds(base + (2 * g + j) * DH, DH), :] = jnp.where(low, top, bottom)


def states_kernel(early, q_ref, k_ref, v_ref, d_ref, state_ref, dq_ref, dk_ref, dv_ref):
    half = state_ref.shape[0] // 2
    packed_state(k_ref, v_ref, state_ref, 0)
    packed_state(q_ref, d_ref, state_ref, half)

    @pl.when(lax.axis_index("ctx") < early)
    def _():
        in_block(q_ref, k_ref, v_ref, d_ref, dq_ref, dk_ref, dv_ref)


def chip_sum_kernel(both_ref, sum_ref):
    half = sum_ref.shape[0]
    core = lax.axis_index("ctx") % 2
    at = pl.ds(pl.multiple_of(core * half, half), half)
    sum_ref[...] = both_ref[0, at, :] + both_ref[1, at, :]


def scan_kernel(chips, lead, part_ref, out_ref):
    rows = part_ref.shape[0]
    each = rows // chips
    core = lax.axis_index("ctx") % 2
    r = lax.broadcasted_iota(jnp.int32, (rows, rows), 0)
    c = lax.broadcasted_iota(jnp.int32, (rows, rows), 1)
    ahead = (r // each + lead) % chips - (c // each + lead) % chips
    ahead = jnp.where(core == 0, ahead, -ahead)
    take = jnp.where((ahead > 0) & (r % each == c % each), 1.0, 0.0).astype(BF16)
    x = part_ref[...]
    high = x.astype(BF16)
    rest = x - high.astype(F32)
    middle = rest.astype(BF16)
    low = (rest - middle.astype(F32)).astype(BF16)
    out_ref[...] = (dot(take, low, NN) + dot(take, middle, NN)) + dot(take, high, NN)


def block_diagonal(packed, g):
    low = low_lanes((DH, PAIR))
    zero = jnp.zeros((PAIR, PAIR), BF16)
    blocks = []
    for j in range(2):
        two = packed[(2 * g + j) * DH : (2 * g + j + 1) * DH]
        blocks.append(
            jnp.concatenate([jnp.where(low, two, 0.0), jnp.where(low, 0.0, two)], axis=0).astype(BF16)
        )
    return jnp.concatenate(
        [
            jnp.concatenate([blocks[0], zero], axis=1),
            jnp.concatenate([zero, blocks[1]], axis=1),
        ],
        axis=0,
    )


def final_kernel(
    early, q_ref, k_ref, v_ref, d_ref, state_ref, carry_ref, iq_ref, ik_ref, iv_ref,
    oq_ref, ok_ref, ov_ref, dq_ref, dk_ref, dv_ref,
):
    half = carry_ref.shape[1]
    width = q_ref.shape[1]
    me = lax.axis_index("ctx")
    core = me % 2

    def finish(sq_ref, sk_ref, sv_ref):
        prefix = carry_ref[0] + jnp.where(core == 1, state_ref[0, :half, :], 0.0)
        suffix = carry_ref[1] + jnp.where(core == 0, state_ref[1, half:, :], 0.0)
        for g in range(width // QUAD):
            at = pl.ds(g * QUAD, QUAD)
            pre, suf = block_diagonal(prefix, g), block_diagonal(suffix, g)
            oq_ref[:, at] = (sq_ref[:, at] + dot(d_ref[:, at], pre, NT)).astype(BF16)
            ok_ref[:, at] = (sk_ref[:, at] + dot(v_ref[:, at], suf, NT)).astype(BF16)
            ov_ref[:, at] = (sv_ref[:, at] + dot(k_ref[:, at], suf, NN)).astype(BF16)

    @pl.when(me < early)
    def _():
        finish(iq_ref, ik_ref, iv_ref)

    @pl.when(me >= early)
    def _():
        in_block(q_ref, k_ref, v_ref, d_ref, dq_ref, dk_ref, dv_ref)
        finish(dq_ref, dk_ref, dv_ref)


def call(kernel, outs, n_in, scratch=(), out_space=VMEM):
    return pl.pallas_call(
        kernel,
        out_shape=outs,
        in_specs=[pl.BlockSpec(memory_space=VMEM)] * n_in,
        out_specs=jax.tree.map(lambda _: pl.BlockSpec(memory_space=out_space), outs),
        scratch_shapes=scratch,
        compiler_params=pltpu.CompilerParams(vmem_limit_bytes=24 * 1024 * 1024),
    )


def body(queries, keys, values, out_grad):
    length, width = queries.shape
    half = width // 2
    count = lax.axis_size("ctx")
    chips = count // 2
    early = count // 2
    lead = chips // 2 + 4
    order = [(s + lead) % chips for s in range(chips)]
    pairs = [[2 * c, 2 * c + 1] for c in range(chips)]
    across = [[2 * c + core for c in order] for core in range(2)]

    wide = jax.ShapeDtypeStruct((length, width), F32)
    state_shape = jax.ShapeDtypeStruct((2 * half, PAIR), F32)
    half_shape = jax.ShapeDtypeStruct((half, PAIR), F32)
    out_shape = jax.ShapeDtypeStruct((length, width), BF16)

    state, iq, ik, iv = call(
        functools.partial(states_kernel, early), (state_shape, wide, wide, wide), 4
    )(queries, keys, values, out_grad)
    both = lax.all_gather(state, "ctx", axis_index_groups=pairs)
    mine = call(chip_sum_kernel, half_shape, 1)(both)

    def exchange(x):
        x = x.reshape(chips, half // chips, PAIR)
        return lax.all_to_all(x, "ctx", 0, 0, axis_index_groups=across).reshape(half, PAIR)

    part = exchange(mine)
    part = call(functools.partial(scan_kernel, chips, lead), half_shape, 1)(part)
    carry = exchange(part)
    carry = lax.all_gather(carry, "ctx", axis_index_groups=pairs)
    return call(
        functools.partial(final_kernel, early),
        (out_shape, out_shape, out_shape),
        9,
        [pltpu.VMEM((length, width), F32)] * 3,
    )(queries, keys, values, out_grad, both, carry, iq, ik, iv)


def solution(mesh):
    spec = P("ctx", "head")
    return jax.shard_map(
        body, mesh=mesh, in_specs=(spec,) * 4, out_specs=(spec,) * 3, check_vma=False
    )
```

```python
import functools

import jax
import jax.numpy as jnp
from jax import lax
from jax.experimental import pallas as pl
from jax.experimental.pallas import tpu as pltpu
from jax.sharding import PartitionSpec as P

DH = 64
PAIR = 2 * DH
QUAD = 4 * DH
VMEM = pltpu.VMEM
F32 = jnp.float32
BF16 = jnp.bfloat16
NT = (((1,), (1,)), ((), ()))
NN = (((1,), (0,)), ((), ()))
TN = (((0,), (0,)), ((), ()))


def dot(a, b, dims):
    return lax.dot_general(a, b, dims, preferred_element_type=F32)


def low_lanes(shape):
    return (lax.broadcasted_iota(jnp.int32, shape, 1) & DH) == 0


def in_block(q_ref, k_ref, v_ref, d_ref, dq_ref, dk_ref, dv_ref):
    length, width = q_ref.shape
    rows = lax.broadcasted_iota(jnp.int32, (length, length), 0)
    cols = lax.broadcasted_iota(jnp.int32, (length, length), 1)
    keep = rows >= cols
    keep_t = cols >= rows
    low = low_lanes((length, PAIR))
    for p in range(width // PAIR):
        at = pl.ds(p * PAIR, PAIR)
        q, k, v, d = q_ref[:, at], k_ref[:, at], v_ref[:, at], d_ref[:, at]
        dq = dk = dv = 0.0
        for mine in (low, ~low):
            kh = jnp.where(mine, k, 0)
            vh = jnp.where(mine, v, 0)
            qh = jnp.where(mine, q, 0)
            dh = jnp.where(mine, d, 0)
            b = jnp.where(keep, dot(d, vh, NT), 0.0).astype(BF16)
            bt = jnp.where(keep_t, dot(v, dh, NT), 0.0).astype(BF16)
            at_ = jnp.where(keep_t, dot(k, qh, NT), 0.0).astype(BF16)
            dq += dot(b, kh, NN)
            dk += dot(bt, qh, NN)
            dv += dot(at_, dh, NN)
        dq_ref[:, at] = dq
        dk_ref[:, at] = dk
        dv_ref[:, at] = dv


def packed_state(a_ref, b_ref, out_ref, base):
    width = a_ref.shape[1]
    low = low_lanes((DH, PAIR))
    for g in range(width // QUAD):
        at = pl.ds(g * QUAD, QUAD)
        full = dot(a_ref[:, at], b_ref[:, at], TN)
        for j in range(2):
            lanes = slice(j * PAIR, (j + 1) * PAIR)
            top = full[j * PAIR : j * PAIR + DH, lanes]
            bottom = full[j * PAIR + DH : (j + 1) * PAIR, lanes]
            out_ref[pl.ds(base + (2 * g + j) * DH, DH), :] = jnp.where(low, top, bottom)


def states_kernel(q_hbm, k_hbm, v_hbm, d_hbm, state_ref, q_ref, k_ref, v_ref, d_ref, sems):
    half = state_ref.shape[0] // 2
    copies = [
        pltpu.make_async_copy(src, dst, sems.at[i])
        for i, (src, dst) in enumerate(
            ((k_hbm, k_ref), (v_hbm, v_ref), (q_hbm, q_ref), (d_hbm, d_ref))
        )
    ]
    for copy in copies:
        copy.start()
    for copy in copies[:2]:
        copy.wait()
    packed_state(k_ref, v_ref, state_ref, 0)
    for copy in copies[2:]:
        copy.wait()
    packed_state(q_ref, d_ref, state_ref, half)


def chip_sum_kernel(
    early, both_ref, q_ref, k_ref, v_ref, d_ref, sum_ref, dq_ref, dk_ref, dv_ref
):
    half = sum_ref.shape[0]
    core = lax.axis_index("ctx") % 2
    at = pl.ds(pl.multiple_of(core * half, half), half)
    sum_ref[...] = both_ref[0, at, :] + both_ref[1, at, :]

    @pl.when(lax.axis_index("ctx") < early)
    def _():
        in_block(q_ref, k_ref, v_ref, d_ref, dq_ref, dk_ref, dv_ref)


def scan_kernel(chips, lead, part_ref, out_ref):
    rows = part_ref.shape[0]
    each = rows // chips
    core = lax.axis_index("ctx") % 2
    r = lax.broadcasted_iota(jnp.int32, (rows, rows), 0)
    c = lax.broadcasted_iota(jnp.int32, (rows, rows), 1)
    ahead = (r // each + lead) % chips - (c // each + lead) % chips
    ahead = jnp.where(core == 0, ahead, -ahead)
    take = jnp.where((ahead > 0) & (r % each == c % each), 1.0, 0.0).astype(BF16)
    x = part_ref[...]
    high = x.astype(BF16)
    rest = x - high.astype(F32)
    middle = rest.astype(BF16)
    low = (rest - middle.astype(F32)).astype(BF16)
    out_ref[...] = (dot(take, low, NN) + dot(take, middle, NN)) + dot(take, high, NN)


def block_diagonal(packed, g):
    low = low_lanes((DH, PAIR))
    zero = jnp.zeros((PAIR, PAIR), BF16)
    blocks = []
    for j in range(2):
        two = packed[(2 * g + j) * DH : (2 * g + j + 1) * DH]
        blocks.append(
            jnp.concatenate([jnp.where(low, two, 0.0), jnp.where(low, 0.0, two)], axis=0).astype(BF16)
        )
    return jnp.concatenate(
        [
            jnp.concatenate([blocks[0], zero], axis=1),
            jnp.concatenate([zero, blocks[1]], axis=1),
        ],
        axis=0,
    )


def final_kernel(
    early, q_ref, k_ref, v_ref, d_ref, state_ref, carry_ref, iq_ref, ik_ref, iv_ref,
    oq_ref, ok_ref, ov_ref, dq_ref, dk_ref, dv_ref,
):
    half = carry_ref.shape[1]
    width = q_ref.shape[1]
    me = lax.axis_index("ctx")
    core = me % 2

    def finish(sq_ref, sk_ref, sv_ref):
        prefix = carry_ref[0] + jnp.where(core == 1, state_ref[0, :half, :], 0.0)
        suffix = carry_ref[1] + jnp.where(core == 0, state_ref[1, half:, :], 0.0)
        for g in range(width // QUAD):
            at = pl.ds(g * QUAD, QUAD)
            pre, suf = block_diagonal(prefix, g), block_diagonal(suffix, g)
            oq_ref[:, at] = (sq_ref[:, at] + dot(d_ref[:, at], pre, NT)).astype(BF16)
            ok_ref[:, at] = (sk_ref[:, at] + dot(v_ref[:, at], suf, NT)).astype(BF16)
            ov_ref[:, at] = (sv_ref[:, at] + dot(k_ref[:, at], suf, NN)).astype(BF16)

    @pl.when(me < early)
    def _():
        finish(iq_ref, ik_ref, iv_ref)

    @pl.when(me >= early)
    def _():
        in_block(q_ref, k_ref, v_ref, d_ref, dq_ref, dk_ref, dv_ref)
        finish(dq_ref, dk_ref, dv_ref)


def call(kernel, outs, n_in, scratch=(), in_space=VMEM, grant=24):
    return pl.pallas_call(
        kernel,
        out_shape=outs,
        in_specs=[pl.BlockSpec(memory_space=in_space)] * n_in,
        out_specs=jax.tree.map(lambda _: pl.BlockSpec(memory_space=VMEM), outs),
        scratch_shapes=scratch,
        compiler_params=pltpu.CompilerParams(vmem_limit_bytes=int(grant * 2**20)),
    )


def body(queries, keys, values, out_grad):
    length, width = queries.shape
    half = width // 2
    count = lax.axis_size("ctx")
    chips = count // 2
    early = count // 2
    lead = chips // 2 + 4
    order = [(s + lead) % chips for s in range(chips)]
    pairs = [[2 * c, 2 * c + 1] for c in range(chips)]
    across = [[2 * c + core for c in order] for core in range(2)]

    wide = jax.ShapeDtypeStruct((length, width), F32)
    state_shape = jax.ShapeDtypeStruct((2 * half, PAIR), F32)
    half_shape = jax.ShapeDtypeStruct((half, PAIR), F32)
    out_shape = jax.ShapeDtypeStruct((length, width), BF16)

    local = (queries, keys, values, out_grad)
    state = call(
        states_kernel,
        state_shape,
        4,
        [pltpu.VMEM((length, width), BF16)] * 4 + [pltpu.SemaphoreType.DMA((4,))],
        in_space=pltpu.HBM,
        grant=53.5,
    )(*local)
    both = lax.all_gather(state, "ctx", axis_index_groups=pairs)
    mine, *partial = call(
        functools.partial(chip_sum_kernel, early), (half_shape,) + (wide,) * 3, 5
    )(both, *local)

    def exchange(x):
        x = x.reshape(chips, half // chips, PAIR)
        return lax.all_to_all(x, "ctx", 0, 0, axis_index_groups=across).reshape(half, PAIR)

    part = exchange(mine)
    part = call(functools.partial(scan_kernel, chips, lead), half_shape, 1)(part)
    carry = exchange(part)
    carry = lax.all_gather(carry, "ctx", axis_index_groups=pairs)
    return call(
        functools.partial(final_kernel, early),
        (out_shape, out_shape, out_shape),
        9,
        [pltpu.VMEM((length, width), F32)] * 3,
    )(*local, both, carry, *partial)


def solution(mesh):
    spec = P("ctx", "head")
    return jax.shard_map(
        body, mesh=mesh, in_specs=(spec,) * 4, out_specs=(spec,) * 3, check_vma=False
    )
```

```python
import functools

import jax
import jax.numpy as jnp
from jax import lax
from jax.experimental import pallas as pl
from jax.experimental.pallas import tpu as pltpu
from jax.sharding import PartitionSpec as P

DH = 64
PAIR = 2 * DH
QUAD = 4 * DH
GRANT = 53.5
VMEM = pltpu.VMEM
F32 = jnp.float32
BF16 = jnp.bfloat16
NT = (((1,), (1,)), ((), ()))
NN = (((1,), (0,)), ((), ()))
TN = (((0,), (0,)), ((), ()))


def dot(a, b, dims):
    return lax.dot_general(a, b, dims, preferred_element_type=F32)


def low_lanes(shape):
    return (lax.broadcasted_iota(jnp.int32, shape, 1) & DH) == 0


def in_block(q_ref, k_ref, v_ref, d_ref, dq_ref, dk_ref, dv_ref):
    length, width = q_ref.shape
    rows = lax.broadcasted_iota(jnp.int32, (length, length), 0)
    cols = lax.broadcasted_iota(jnp.int32, (length, length), 1)
    keep = rows >= cols
    keep_t = cols >= rows
    low = low_lanes((length, PAIR))

    def pair(p, _):
        at = pl.ds(p * PAIR, PAIR)
        q, k, v, d = q_ref[:, at], k_ref[:, at], v_ref[:, at], d_ref[:, at]
        dq = dk = dv = 0.0
        for mine in (low, ~low):
            kh = jnp.where(mine, k, 0)
            vh = jnp.where(mine, v, 0)
            qh = jnp.where(mine, q, 0)
            dh = jnp.where(mine, d, 0)
            b = jnp.where(keep, dot(d, vh, NT), 0.0).astype(BF16)
            bt = jnp.where(keep_t, dot(v, dh, NT), 0.0).astype(BF16)
            at_ = jnp.where(keep_t, dot(k, qh, NT), 0.0).astype(BF16)
            dq += dot(b, kh, NN)
            dk += dot(bt, qh, NN)
            dv += dot(at_, dh, NN)
        dq_ref[:, at] = dq
        dk_ref[:, at] = dk
        dv_ref[:, at] = dv
        return 0

    [pair(p, 0) for p in range(width // PAIR)]


def packed_state(a_ref, b_ref, mine, own_ref, send_ref):
    width = a_ref.shape[1]
    low = low_lanes((DH, PAIR))
    blocks = []
    for g in range(width // QUAD):
        at = pl.ds(g * QUAD, QUAD)
        full = dot(a_ref[:, at], b_ref[:, at], TN)
        for j in range(2):
            lanes = slice(j * PAIR, (j + 1) * PAIR)
            top = full[j * PAIR : j * PAIR + DH, lanes]
            bottom = full[j * PAIR + DH : (j + 1) * PAIR, lanes]
            blocks.append(jnp.where(low, top, bottom))

    def store(ref):
        for p, block in enumerate(blocks):
            ref[pl.ds(p * DH, DH), :] = block

    pl.when(mine)(functools.partial(store, own_ref))
    pl.when(jnp.logical_not(mine))(functools.partial(store, send_ref))


def states_kernel(
    q_hbm, k_hbm, v_hbm, d_hbm, own_ref, send_ref, q_ref, k_ref, v_ref, d_ref, sems
):
    core = lax.axis_index("ctx") % 2
    copies = [
        pltpu.make_async_copy(src, dst, sems.at[i])
        for i, (src, dst) in enumerate(
            ((k_hbm, k_ref), (v_hbm, v_ref), (q_hbm, q_ref), (d_hbm, d_ref))
        )
    ]
    for copy in copies:
        copy.start()
    for copy in copies[:2]:
        copy.wait()
    packed_state(k_ref, v_ref, core == 0, own_ref, send_ref)
    for copy in copies[2:]:
        copy.wait()
    packed_state(q_ref, d_ref, core == 1, own_ref, send_ref)


def chip_sum_kernel(
    early, own_ref, sent_ref, q_ref, k_ref, v_ref, d_ref, sum_ref, dq_ref, dk_ref, dv_ref
):
    core = lax.axis_index("ctx") % 2
    sum_ref[...] = own_ref[...] + sent_ref[1 - core]

    @pl.when(lax.axis_index("ctx") < early)
    def _():
        in_block(q_ref, k_ref, v_ref, d_ref, dq_ref, dk_ref, dv_ref)


def add_own_kernel(carry_ref, own_ref, out_ref):
    out_ref[...] = carry_ref[...] + own_ref[...]


def scan_kernel(order, part_ref, out_ref):
    chips = len(order)
    each = part_ref.shape[0] // chips
    slot = {chip: s for s, chip in enumerate(order)}

    def scan(sequence):
        total = jnp.zeros((each, PAIR), F32)
        for chip in sequence:
            at = pl.ds(slot[chip] * each, each)
            out_ref[at, :] = total
            total = total + part_ref[at, :]

    core = lax.axis_index("ctx") % 2

    @pl.when(core == 0)
    def _():
        scan(range(chips))

    @pl.when(core == 1)
    def _():
        scan(reversed(range(chips)))


def block_diagonal(packed, g):
    low = low_lanes((DH, PAIR))
    zero = jnp.zeros((PAIR, PAIR), BF16)
    blocks = []
    for j in range(2):
        two = packed[(2 * g + j) * DH : (2 * g + j + 1) * DH]
        blocks.append(
            jnp.concatenate([jnp.where(low, two, 0.0), jnp.where(low, 0.0, two)], axis=0).astype(BF16)
        )
    return jnp.concatenate(
        [
            jnp.concatenate([blocks[0], zero], axis=1),
            jnp.concatenate([zero, blocks[1]], axis=1),
        ],
        axis=0,
    )


def final_kernel(
    early, q_ref, k_ref, v_ref, d_ref, carry_ref, other_ref, iq_ref, ik_ref, iv_ref,
    oq_hbm, ok_hbm, ov_hbm, dq_ref, dk_ref, dv_ref, oq_ref, ok_ref, ov_ref, sems,
):
    width = q_ref.shape[1]
    me = lax.axis_index("ctx")
    core = me % 2

    def finish(sq_ref, sk_ref, sv_ref):
        prefix = jnp.where(core == 0, carry_ref[...], other_ref[0])
        suffix = jnp.where(core == 1, carry_ref[...], other_ref[1])
        copies = []
        for g in range(width // QUAD):
            at = pl.ds(g * QUAD, QUAD)
            pre, suf = block_diagonal(prefix, g), block_diagonal(suffix, g)
            for i, (own, sum_ref, x_ref, state, dims, hbm) in enumerate((
                (oq_ref, sq_ref, d_ref, pre, NT, oq_hbm),
                (ok_ref, sk_ref, v_ref, suf, NT, ok_hbm),
                (ov_ref, sv_ref, k_ref, suf, NN, ov_hbm),
            )):
                own[:, at] = (sum_ref[:, at] + dot(x_ref[:, at], state, dims)).astype(BF16)
                copy = pltpu.make_async_copy(own.at[:, at], hbm.at[:, at], sems.at[i, g])
                copy.start()
                copies.append(copy)
        for copy in copies:
            copy.wait()

    @pl.when(me < early)
    def _():
        finish(iq_ref, ik_ref, iv_ref)

    @pl.when(me >= early)
    def _():
        in_block(q_ref, k_ref, v_ref, d_ref, dq_ref, dk_ref, dv_ref)
        finish(dq_ref, dk_ref, dv_ref)


def call(kernel, outs, n_in, scratch=(), in_space=VMEM, out_space=VMEM, grant=24):
    return pl.pallas_call(
        kernel,
        out_shape=outs,
        in_specs=[pl.BlockSpec(memory_space=in_space)] * n_in,
        out_specs=jax.tree.map(lambda _: pl.BlockSpec(memory_space=out_space), outs),
        scratch_shapes=scratch,
        compiler_params=pltpu.CompilerParams(vmem_limit_bytes=int(grant * 2**20)),
    )


def body(queries, keys, values, out_grad):
    length, width = queries.shape
    half = width // 2
    count = lax.axis_size("ctx")
    chips = count // 2
    early = count // 2
    lead = chips // 2 + 4
    order = [(s + lead) % chips for s in range(chips)]
    pairs = [[2 * c, 2 * c + 1] for c in range(chips)]
    across = [[2 * c + core for c in order] for core in range(2)]

    wide = jax.ShapeDtypeStruct((length, width), F32)
    half_shape = jax.ShapeDtypeStruct((half, PAIR), F32)
    out_shape = jax.ShapeDtypeStruct((length, width), BF16)

    local = (queries, keys, values, out_grad)
    own, send = call(
        states_kernel,
        (half_shape, half_shape),
        4,
        [pltpu.VMEM((length, width), BF16)] * 4 + [pltpu.SemaphoreType.DMA((4,))],
        in_space=pltpu.HBM,
        grant=GRANT,
    )(*local)
    sent = lax.all_gather(send, "ctx", axis_index_groups=pairs)
    mine, *partial = call(
        functools.partial(chip_sum_kernel, early), (half_shape,) + (wide,) * 3, 6
    )(own, sent, *local)

    def exchange(x):
        x = x.reshape(chips, half // chips, PAIR)
        return lax.all_to_all(x, "ctx", 0, 0, axis_index_groups=across).reshape(half, PAIR)

    part = exchange(mine)
    part = call(functools.partial(scan_kernel, order), half_shape, 1)(part)
    carry = exchange(part)
    other = call(add_own_kernel, half_shape, 2)(carry, own)
    other = lax.all_gather(other, "ctx", axis_index_groups=pairs)
    return call(
        functools.partial(final_kernel, early),
        (out_shape, out_shape, out_shape),
        9,
        [pltpu.VMEM((length, width), F32)] * 3
        + [pltpu.VMEM((length, width), BF16)] * 3
        + [pltpu.SemaphoreType.DMA((3, width // QUAD))],
        out_space=pltpu.HBM,
    )(*local, carry, other, *partial)


def solution(mesh):
    spec = P("ctx", "head")
    return jax.shard_map(
        body, mesh=mesh, in_specs=(spec,) * 4, out_specs=(spec,) * 3, check_vma=False
    )
```

```python
import functools

import jax
import jax.numpy as jnp
from jax import lax
from jax.experimental import pallas as pl
from jax.experimental.pallas import tpu as pltpu
from jax.sharding import PartitionSpec as P

DH = 64
PAIR = 2 * DH
QUAD = 4 * DH
GRANT = 53.5
VMEM = pltpu.VMEM
F32 = jnp.float32
BF16 = jnp.bfloat16
NT = (((1,), (1,)), ((), ()))
NN = (((1,), (0,)), ((), ()))
TN = (((0,), (0,)), ((), ()))


def dot(a, b, dims):
    return lax.dot_general(a, b, dims, preferred_element_type=F32)


def low_lanes(shape):
    return (lax.broadcasted_iota(jnp.int32, shape, 1) & DH) == 0


def in_block(q_ref, k_ref, v_ref, d_ref, dq_ref, dk_ref, dv_ref):
    length, width = q_ref.shape
    rows = lax.broadcasted_iota(jnp.int32, (length, length), 0)
    cols = lax.broadcasted_iota(jnp.int32, (length, length), 1)
    keep = rows >= cols
    keep_t = cols >= rows
    low = low_lanes((length, PAIR))

    def pair(p, _):
        at = pl.ds(p * PAIR, PAIR)
        q, k, v, d = q_ref[:, at], k_ref[:, at], v_ref[:, at], d_ref[:, at]
        dq = dk = dv = 0.0
        for mine in (low, ~low):
            kh = jnp.where(mine, k, 0)
            vh = jnp.where(mine, v, 0)
            qh = jnp.where(mine, q, 0)
            dh = jnp.where(mine, d, 0)
            b = jnp.where(keep, dot(d, vh, NT), 0.0).astype(BF16)
            bt = jnp.where(keep_t, dot(v, dh, NT), 0.0).astype(BF16)
            at_ = jnp.where(keep_t, dot(k, qh, NT), 0.0).astype(BF16)
            dq += dot(b, kh, NN)
            dk += dot(bt, qh, NN)
            dv += dot(at_, dh, NN)
        dq_ref[:, at] = dq
        dk_ref[:, at] = dk
        dv_ref[:, at] = dv
        return 0

    [pair(p, 0) for p in range(width // PAIR)]


def packed_state(a_ref, b_ref, mine, own_ref, send_ref):
    width = a_ref.shape[1]
    low = low_lanes((DH, PAIR))
    blocks = []
    for g in range(width // QUAD):
        at = pl.ds(g * QUAD, QUAD)
        full = dot(a_ref[:, at], b_ref[:, at], TN)
        for j in range(2):
            lanes = slice(j * PAIR, (j + 1) * PAIR)
            top = full[j * PAIR : j * PAIR + DH, lanes]
            bottom = full[j * PAIR + DH : (j + 1) * PAIR, lanes]
            blocks.append(jnp.where(low, top, bottom))

    def store(ref):
        for p, block in enumerate(blocks):
            ref[pl.ds(p * DH, DH), :] = block

    pl.when(mine)(functools.partial(store, own_ref))
    pl.when(jnp.logical_not(mine))(functools.partial(store, send_ref))


def states_kernel(
    q_hbm, k_hbm, v_hbm, d_hbm, own_ref, send_ref, q_ref, k_ref, v_ref, d_ref, sems
):
    core = lax.axis_index("ctx") % 2
    copies = [
        pltpu.make_async_copy(src, dst, sems.at[i])
        for i, (src, dst) in enumerate(
            ((k_hbm, k_ref), (v_hbm, v_ref), (q_hbm, q_ref), (d_hbm, d_ref))
        )
    ]
    for copy in copies:
        copy.start()
    for copy in copies[:2]:
        copy.wait()
    packed_state(k_ref, v_ref, core == 0, own_ref, send_ref)
    for copy in copies[2:]:
        copy.wait()
    packed_state(q_ref, d_ref, core == 1, own_ref, send_ref)


def chip_sum_kernel(
    early, own_ref, sent_ref, q_ref, k_ref, v_ref, d_ref, sum_ref, dq_ref, dk_ref, dv_ref
):
    core = lax.axis_index("ctx") % 2
    sum_ref[...] = own_ref[...] + sent_ref[1 - core]

    @pl.when(lax.axis_index("ctx") < early)
    def _():
        in_block(q_ref, k_ref, v_ref, d_ref, dq_ref, dk_ref, dv_ref)


def scan_kernel(order, part_ref, out_ref):
    chips = len(order)
    each = part_ref.shape[0] // chips
    slot = {chip: s for s, chip in enumerate(order)}

    def scan(sequence):
        total = jnp.zeros((each, PAIR), F32)
        for chip in sequence:
            at = pl.ds(slot[chip] * each, each)
            out_ref[at, :] = total
            total = total + part_ref[at, :]

    core = lax.axis_index("ctx") % 2

    @pl.when(core == 0)
    def _():
        scan(range(chips))

    @pl.when(core == 1)
    def _():
        scan(reversed(range(chips)))


def block_diagonal(packed, g):
    low = low_lanes((DH, PAIR))
    zero = jnp.zeros((PAIR, PAIR), BF16)
    blocks = []
    for j in range(2):
        two = packed[(2 * g + j) * DH : (2 * g + j + 1) * DH]
        blocks.append(
            jnp.concatenate([jnp.where(low, two, 0.0), jnp.where(low, 0.0, two)], axis=0).astype(BF16)
        )
    return jnp.concatenate(
        [
            jnp.concatenate([blocks[0], zero], axis=1),
            jnp.concatenate([zero, blocks[1]], axis=1),
        ],
        axis=0,
    )


def add_own_kernel(
    early, carry_ref, own_ref, k_ref, v_ref, ik_ref, iv_ref, out_ref, rk_ref, rv_ref
):
    out_ref[...] = carry_ref[...] + own_ref[...]
    me = lax.axis_index("ctx")

    @pl.when((me < early) & (me % 2 == 1))
    def _():
        suffix = carry_ref[...]
        for g in range(k_ref.shape[1] // QUAD):
            at = pl.ds(g * QUAD, QUAD)
            suf = block_diagonal(suffix, g)
            rk_ref[:, at] = (ik_ref[:, at] + dot(v_ref[:, at], suf, NT)).astype(BF16)
            rv_ref[:, at] = (iv_ref[:, at] + dot(k_ref[:, at], suf, NN)).astype(BF16)


def final_kernel(
    early, q_ref, k_ref, v_ref, d_ref, carry_ref, other_ref, iq_ref, ik_ref, iv_ref,
    rk_ref, rv_ref,
    oq_hbm, ok_hbm, ov_hbm, dq_ref, dk_ref, dv_ref, oq_ref, ok_ref, ov_ref, sems,
):
    width = q_ref.shape[1]
    me = lax.axis_index("ctx")
    core = me % 2

    def finish(sq_ref, sk_ref, sv_ref):
        prefix = jnp.where(core == 0, carry_ref[...], other_ref[0])
        suffix = jnp.where(core == 1, carry_ref[...], other_ref[1])
        copies = []
        for g in range(width // QUAD):
            at = pl.ds(g * QUAD, QUAD)
            pre, suf = block_diagonal(prefix, g), block_diagonal(suffix, g)
            for i, (own, sum_ref, x_ref, state, dims, hbm) in enumerate((
                (oq_ref, sq_ref, d_ref, pre, NT, oq_hbm),
                (ok_ref, sk_ref, v_ref, suf, NT, ok_hbm),
                (ov_ref, sv_ref, k_ref, suf, NN, ov_hbm),
            )):
                own[:, at] = (sum_ref[:, at] + dot(x_ref[:, at], state, dims)).astype(BF16)
                copy = pltpu.make_async_copy(own.at[:, at], hbm.at[:, at], sems.at[i, g])
                copy.start()
                copies.append(copy)
        for copy in copies:
            copy.wait()

    @pl.when((me < early) & (core == 1))
    def _():
        copies = [
            pltpu.make_async_copy(rk_ref, ok_hbm, sems.at[1, 0]),
            pltpu.make_async_copy(rv_ref, ov_hbm, sems.at[2, 0]),
        ]
        for copy in copies:
            copy.start()
        prefix = other_ref[0]
        for g in range(width // QUAD):
            at = pl.ds(g * QUAD, QUAD)
            pre = block_diagonal(prefix, g)
            oq_ref[:, at] = (iq_ref[:, at] + dot(d_ref[:, at], pre, NT)).astype(BF16)
            copy = pltpu.make_async_copy(oq_ref.at[:, at], oq_hbm.at[:, at], sems.at[0, g])
            copy.start()
            copies.append(copy)
        for copy in copies:
            copy.wait()

    @pl.when((me < early) & (core == 0))
    def _():
        finish(iq_ref, ik_ref, iv_ref)

    @pl.when(me >= early)
    def _():
        in_block(q_ref, k_ref, v_ref, d_ref, dq_ref, dk_ref, dv_ref)
        finish(dq_ref, dk_ref, dv_ref)


def call(kernel, outs, n_in, scratch=(), in_space=VMEM, out_space=VMEM, grant=24):
    return pl.pallas_call(
        kernel,
        out_shape=outs,
        in_specs=[pl.BlockSpec(memory_space=in_space)] * n_in,
        out_specs=jax.tree.map(lambda _: pl.BlockSpec(memory_space=out_space), outs),
        scratch_shapes=scratch,
        compiler_params=pltpu.CompilerParams(vmem_limit_bytes=int(grant * 2**20)),
    )


def body(queries, keys, values, out_grad):
    length, width = queries.shape
    half = width // 2
    count = lax.axis_size("ctx")
    chips = count // 2
    early = count // 2
    lead = chips // 2 + 4
    order = [(s + lead) % chips for s in range(chips)]
    pairs = [[2 * c, 2 * c + 1] for c in range(chips)]
    across = [[2 * c + core for c in order] for core in range(2)]

    wide = jax.ShapeDtypeStruct((length, width), F32)
    half_shape = jax.ShapeDtypeStruct((half, PAIR), F32)
    out_shape = jax.ShapeDtypeStruct((length, width), BF16)

    local = (queries, keys, values, out_grad)
    own, send = call(
        states_kernel,
        (half_shape, half_shape),
        4,
        [pltpu.VMEM((length, width), BF16)] * 4 + [pltpu.SemaphoreType.DMA((4,))],
        in_space=pltpu.HBM,
        grant=GRANT,
    )(*local)
    sent = lax.all_gather(send, "ctx", axis_index_groups=pairs)
    mine, *partial = call(
        functools.partial(chip_sum_kernel, early), (half_shape,) + (wide,) * 3, 6
    )(own, sent, *local)

    def exchange(x):
        x = x.reshape(chips, half // chips, PAIR)
        return lax.all_to_all(x, "ctx", 0, 0, axis_index_groups=across).reshape(half, PAIR)

    part = exchange(mine)
    part = call(functools.partial(scan_kernel, order), half_shape, 1)(part)
    carry = exchange(part)
    other, *ready = call(
        functools.partial(add_own_kernel, early), (half_shape, out_shape, out_shape), 6
    )(carry, own, keys, values, *partial[1:])
    other = lax.all_gather(other, "ctx", axis_index_groups=pairs)
    return call(
        functools.partial(final_kernel, early),
        (out_shape, out_shape, out_shape),
        11,
        [pltpu.VMEM((length, width), F32)] * 3
        + [pltpu.VMEM((length, width), BF16)] * 3
        + [pltpu.SemaphoreType.DMA((3, width // QUAD))],
        out_space=pltpu.HBM,
    )(*local, carry, other, *partial, *ready)


def solution(mesh):
    spec = P("ctx", "head")
    return jax.shard_map(
        body, mesh=mesh, in_specs=(spec,) * 4, out_specs=(spec,) * 3, check_vma=False
    )
```

```python
import functools

import jax
import jax.numpy as jnp
from jax import lax
from jax.experimental import pallas as pl
from jax.experimental.pallas import tpu as pltpu
from jax.sharding import PartitionSpec as P

DH = 64
PAIR = 2 * DH
QUAD = 4 * DH
GRANT = 53.5
VMEM = pltpu.VMEM
F32 = jnp.float32
BF16 = jnp.bfloat16
NT = (((1,), (1,)), ((), ()))
NN = (((1,), (0,)), ((), ()))
TN = (((0,), (0,)), ((), ()))


def dot(a, b, dims):
    return lax.dot_general(a, b, dims, preferred_element_type=F32)


def low_lanes(shape):
    return (lax.broadcasted_iota(jnp.int32, shape, 1) & DH) == 0


def in_block(q_ref, k_ref, v_ref, d_ref, dq_ref, dk_ref, dv_ref):
    length, width = q_ref.shape
    rows = lax.broadcasted_iota(jnp.int32, (length, length), 0)
    cols = lax.broadcasted_iota(jnp.int32, (length, length), 1)
    keep = rows >= cols
    keep_t = cols >= rows
    low = low_lanes((length, PAIR))

    def pair(p, _):
        at = pl.ds(p * PAIR, PAIR)
        q, k, v, d = q_ref[:, at], k_ref[:, at], v_ref[:, at], d_ref[:, at]
        dq = dk = dv = 0.0
        for mine in (low, ~low):
            kh = jnp.where(mine, k, 0)
            vh = jnp.where(mine, v, 0)
            qh = jnp.where(mine, q, 0)
            dh = jnp.where(mine, d, 0)
            b = jnp.where(keep, dot(d, vh, NT), 0.0).astype(BF16)
            bt = jnp.where(keep_t, dot(v, dh, NT), 0.0).astype(BF16)
            at_ = jnp.where(keep_t, dot(k, qh, NT), 0.0).astype(BF16)
            dq += dot(b, kh, NN)
            dk += dot(bt, qh, NN)
            dv += dot(at_, dh, NN)
        dq_ref[:, at] = dq
        dk_ref[:, at] = dk
        dv_ref[:, at] = dv
        return 0

    [pair(p, 0) for p in range(width // PAIR)]


def packed_state(a_ref, b_ref, mine, own_ref, send_ref):
    width = a_ref.shape[1]
    low = low_lanes((DH, PAIR))
    blocks = []
    for g in range(width // QUAD):
        at = pl.ds(g * QUAD, QUAD)
        full = dot(a_ref[:, at], b_ref[:, at], TN)
        for j in range(2):
            lanes = slice(j * PAIR, (j + 1) * PAIR)
            top = full[j * PAIR : j * PAIR + DH, lanes]
            bottom = full[j * PAIR + DH : (j + 1) * PAIR, lanes]
            blocks.append(jnp.where(low, top, bottom))

    def store(ref):
        for p, block in enumerate(blocks):
            ref[pl.ds(p * DH, DH), :] = block

    pl.when(mine)(functools.partial(store, own_ref))
    pl.when(jnp.logical_not(mine))(functools.partial(store, send_ref))


def states_kernel(
    q_hbm, k_hbm, v_hbm, d_hbm, own_ref, send_ref, q_ref, k_ref, v_ref, d_ref, sems
):
    core = lax.axis_index("ctx") % 2
    copies = [
        pltpu.make_async_copy(src, dst, sems.at[i])
        for i, (src, dst) in enumerate(
            ((k_hbm, k_ref), (v_hbm, v_ref), (q_hbm, q_ref), (d_hbm, d_ref))
        )
    ]
    for copy in copies:
        copy.start()
    for copy in copies[:2]:
        copy.wait()
    packed_state(k_ref, v_ref, core == 0, own_ref, send_ref)
    for copy in copies[2:]:
        copy.wait()
    packed_state(q_ref, d_ref, core == 1, own_ref, send_ref)


def chip_sum_kernel(
    early, own_ref, sent_ref, q_ref, k_ref, v_ref, d_ref, sum_ref, dq_ref, dk_ref, dv_ref
):
    core = lax.axis_index("ctx") % 2
    sum_ref[...] = own_ref[...] + sent_ref[1 - core]

    @pl.when(lax.axis_index("ctx") < early)
    def _():
        in_block(q_ref, k_ref, v_ref, d_ref, dq_ref, dk_ref, dv_ref)


def scan_kernel(orders, part_ref, out_ref):
    chips = len(orders[0])
    each = part_ref.shape[0] // chips
    slots = [{chip: s for s, chip in enumerate(order)} for order in orders]

    def scan(slot, sequence):
        total = jnp.zeros((each, PAIR), F32)
        for chip in sequence:
            at = pl.ds(slot[chip] * each, each)
            out_ref[at, :] = total
            total = total + part_ref[at, :]

    core = lax.axis_index("ctx") % 2

    @pl.when(core == 0)
    def _():
        scan(slots[0], range(chips))

    @pl.when(core == 1)
    def _():
        scan(slots[1], reversed(range(chips)))


def block_diagonal(packed, g):
    low = low_lanes((DH, PAIR))
    zero = jnp.zeros((PAIR, PAIR), BF16)
    blocks = []
    for j in range(2):
        two = packed[(2 * g + j) * DH : (2 * g + j + 1) * DH]
        blocks.append(
            jnp.concatenate([jnp.where(low, two, 0.0), jnp.where(low, 0.0, two)], axis=0).astype(BF16)
        )
    return jnp.concatenate(
        [
            jnp.concatenate([blocks[0], zero], axis=1),
            jnp.concatenate([zero, blocks[1]], axis=1),
        ],
        axis=0,
    )


def add_own_kernel(
    early, carry_ref, own_ref, k_ref, v_ref, ik_ref, iv_ref, out_ref, rk_ref, rv_ref
):
    out_ref[...] = carry_ref[...] + own_ref[...]
    me = lax.axis_index("ctx")

    @pl.when((me < early) & (me % 2 == 1))
    def _():
        suffix = carry_ref[...]
        for g in range(k_ref.shape[1] // QUAD):
            at = pl.ds(g * QUAD, QUAD)
            suf = block_diagonal(suffix, g)
            rk_ref[:, at] = (ik_ref[:, at] + dot(v_ref[:, at], suf, NT)).astype(BF16)
            rv_ref[:, at] = (iv_ref[:, at] + dot(k_ref[:, at], suf, NN)).astype(BF16)


def final_kernel(
    early, q_ref, k_ref, v_ref, d_ref, carry_ref, other_ref, iq_ref, ik_ref, iv_ref,
    rk_ref, rv_ref,
    oq_hbm, ok_hbm, ov_hbm, dq_ref, dk_ref, dv_ref, oq_ref, ok_ref, ov_ref, sems,
):
    width = q_ref.shape[1]
    me = lax.axis_index("ctx")
    core = me % 2

    def finish(sq_ref, sk_ref, sv_ref):
        prefix = jnp.where(core == 0, carry_ref[...], other_ref[0])
        suffix = jnp.where(core == 1, carry_ref[...], other_ref[1])
        copies = []
        for g in range(width // QUAD):
            at = pl.ds(g * QUAD, QUAD)
            pre, suf = block_diagonal(prefix, g), block_diagonal(suffix, g)
            for i, (own, sum_ref, x_ref, state, dims, hbm) in enumerate((
                (oq_ref, sq_ref, d_ref, pre, NT, oq_hbm),
                (ok_ref, sk_ref, v_ref, suf, NT, ok_hbm),
                (ov_ref, sv_ref, k_ref, suf, NN, ov_hbm),
            )):
                own[:, at] = (sum_ref[:, at] + dot(x_ref[:, at], state, dims)).astype(BF16)
                copy = pltpu.make_async_copy(own.at[:, at], hbm.at[:, at], sems.at[i, g])
                copy.start()
                copies.append(copy)
        for copy in copies:
            copy.wait()

    @pl.when((me < early) & (core == 1))
    def _():
        copies = [
            pltpu.make_async_copy(rk_ref, ok_hbm, sems.at[1, 0]),
            pltpu.make_async_copy(rv_ref, ov_hbm, sems.at[2, 0]),
        ]
        for copy in copies:
            copy.start()
        prefix = other_ref[0]
        for g in range(width // QUAD):
            at = pl.ds(g * QUAD, QUAD)
            pre = block_diagonal(prefix, g)
            oq_ref[:, at] = (iq_ref[:, at] + dot(d_ref[:, at], pre, NT)).astype(BF16)
            copy = pltpu.make_async_copy(oq_ref.at[:, at], oq_hbm.at[:, at], sems.at[0, g])
            copy.start()
            copies.append(copy)
        for copy in copies:
            copy.wait()

    @pl.when((me < early) & (core == 0))
    def _():
        finish(iq_ref, ik_ref, iv_ref)

    @pl.when(me >= early)
    def _():
        in_block(q_ref, k_ref, v_ref, d_ref, dq_ref, dk_ref, dv_ref)
        finish(dq_ref, dk_ref, dv_ref)


def call(kernel, outs, n_in, scratch=(), in_space=VMEM, out_space=VMEM, grant=24):
    return pl.pallas_call(
        kernel,
        out_shape=outs,
        in_specs=[pl.BlockSpec(memory_space=in_space)] * n_in,
        out_specs=jax.tree.map(lambda _: pl.BlockSpec(memory_space=out_space), outs),
        scratch_shapes=scratch,
        compiler_params=pltpu.CompilerParams(vmem_limit_bytes=int(grant * 2**20)),
    )


def body(queries, keys, values, out_grad):
    length, width = queries.shape
    half = width // 2
    count = lax.axis_size("ctx")
    chips = count // 2
    early = count // 2
    leads = (chips // 2 + 4, chips * 3 // 4 + 4)
    orders = [[(s + lead) % chips for s in range(chips)] for lead in leads]
    pairs = [[2 * c, 2 * c + 1] for c in range(chips)]
    across = [[2 * c + core for c in orders[core]] for core in range(2)]

    wide = jax.ShapeDtypeStruct((length, width), F32)
    half_shape = jax.ShapeDtypeStruct((half, PAIR), F32)
    out_shape = jax.ShapeDtypeStruct((length, width), BF16)

    local = (queries, keys, values, out_grad)
    own, send = call(
        states_kernel,
        (half_shape, half_shape),
        4,
        [pltpu.VMEM((length, width), BF16)] * 4 + [pltpu.SemaphoreType.DMA((4,))],
        in_space=pltpu.HBM,
        grant=GRANT,
    )(*local)
    sent = lax.all_gather(send, "ctx", axis_index_groups=pairs)
    mine, *partial = call(
        functools.partial(chip_sum_kernel, early), (half_shape,) + (wide,) * 3, 6
    )(own, sent, *local)

    def exchange(x):
        x = x.reshape(chips, half // chips, PAIR)
        return lax.all_to_all(x, "ctx", 0, 0, axis_index_groups=across).reshape(half, PAIR)

    part = exchange(mine)
    part = call(functools.partial(scan_kernel, orders), half_shape, 1)(part)
    carry = exchange(part)
    other, *ready = call(
        functools.partial(add_own_kernel, early), (half_shape, out_shape, out_shape), 6
    )(carry, own, keys, values, *partial[1:])
    other = lax.all_gather(other, "ctx", axis_index_groups=pairs)
    return call(
        functools.partial(final_kernel, early),
        (out_shape, out_shape, out_shape),
        11,
        [pltpu.VMEM((length, width), F32)] * 3
        + [pltpu.VMEM((length, width), BF16)] * 3
        + [pltpu.SemaphoreType.DMA((3, width // QUAD))],
        out_space=pltpu.HBM,
    )(*local, carry, other, *partial, *ready)


def solution(mesh):
    spec = P("ctx", "head")
    return jax.shard_map(
        body, mesh=mesh, in_specs=(spec,) * 4, out_specs=(spec,) * 3, check_vma=False
    )
```
